256 devices in a mesh: aux: 32 (over y, z), occ: 8 (over x, core).
Axes of the slice: x: 4, y: 4, z: 8, core: 2. Of those that a mesh axis runs over, the one named last changes fastest.
Arguments:
- three_index: bfloat16 [32, 2048, 128, 128], P('occ', 'aux'), may hold values from -6 to 6
- occ_coeff: bfloat16 [1024, 256], replicated, may hold values from -0.375 to 0.375
- occ_mask: int32 [8, 8], replicated, may hold values 0 or 1
- screen_list: int32 [32, 32], P('aux', 'occ'), may hold values from 0 to 7, as said below
- screen_count: int32 [32, 8], P('aux', 'occ'), may hold values from 1 to 4, as said below
- owner_order: int32 [64], replicated, may hold values from 0 to 63, each once
Outputs:
- exchange: float32 [64, 128, 128], P('aux', 'occ')
The draws below stay inside these ranges and needn't reach their ends.
Inputs may be any that keep to these rules, and one draw needn't show every extreme that they name: `screen_list`: the 4 entries of one aux index and one first-index block are distinct basis blocks. `screen_count`: slots below the count are live; in every aux index some first-index block has all 4 slots live.
All inputs are finite; a program needn't handle non-finite values.
Results may differ from the reference program's by a relative error of at most 0.0003.
Values may be sent and summed in bfloat16 or wider, within the bound.
A program may use at most 64 MiB of HBM per device.

```python
import math
import jax
import jax.numpy as jnp
from jax import lax

BLOCK = 128
AUX_DEV = 64
OCC_DEV = 32
SLOTS = 4
NBLOCKS = 8
NBASIS = 1024
AUX_ALL = 2048
ORBITALS = 256
PAIRS = 64
N_AUX = 32
N_OCC = 8


def draw_screen_list(key, part):
    key = jax.random.fold_in(key, 11)
    scores = jax.random.randint(key, (N_AUX * NBLOCKS, NBLOCKS), 0, 1 << 20) * NBLOCKS
    scores = scores + jnp.arange(NBLOCKS, dtype=jnp.int32)[None, :]
    picked = jnp.argsort(scores, axis=1)[:, :SLOTS]
    return picked.reshape(N_AUX, NBLOCKS * SLOTS).astype(jnp.int32)


def draw_screen_count(key, part):
    key = jax.random.fold_in(key, 23)
    first_key, second_key = jax.random.split(key)
    base = jax.random.randint(first_key, (N_AUX, NBLOCKS), 1, SLOTS // 2 + 1)
    busiest = jax.random.randint(second_key, (N_AUX, 1), 0, NBLOCKS)
    column = jnp.arange(NBLOCKS, dtype=jnp.int32)[None, :]
    return jnp.where(column == busiest, SLOTS, base).astype(jnp.int32)


def place_ends(drawn, own_key, least, largest):
    dims = drawn.shape
    spot = [jax.random.randint(jax.random.fold_in(own_key, axis), (), 0, dims[axis]) for axis in range(len(dims))]
    drawn = drawn.at[tuple(spot)].set(least)
    longest = dims.index(max(dims))
    spot[longest] = (spot[longest] + 1) % dims[longest]
    return drawn.at[tuple(spot)].set(largest)


def block_scale(own_key, shape, shards, smallest, largest):
    def one(position, shards_of):
        heights = jax.random.uniform(jax.random.fold_in(jax.random.fold_in(own_key, 6), position), (shards_of,), jnp.float32, smallest / len(shards), largest / len(shards))
        return jnp.repeat(jnp.exp(heights), shape[position] // shards_of).reshape((-1,) + (1,) * (len(shape) - position - 1))

    gain = one(*shards[0])
    for cut in shards[1:]:
        gain = gain * one(*cut)
    return gain


def noise(rng, dims, deviation, reach, cuts=(), kind=jnp.bfloat16):
    values = jax.random.normal(rng, dims, jnp.float32) * deviation
    if len(cuts) > 0:
        values = block_scale(rng, dims, cuts, -0.22, 0.18) * values
    return jnp.clip(values, min=-reach, max=reach).astype(kind)


def setup_inputs(seed: int = 0) -> dict:
    seeds = jax.random.split(jax.random.key(seed), 7)
    three_index = noise(seeds[0], (NBLOCKS * SLOTS, AUX_ALL, BLOCK, BLOCK), 1.0, 6.0, ((0, 8), (1, 32)))
    occ_coeff = noise(seeds[1], (NBASIS, ORBITALS), (2 * BLOCK) ** -0.5, 0.375)
    occ_mask = place_ends((jax.random.randint(seeds[2], (NBLOCKS, N_OCC), 0, 4) < 3).astype(jnp.int32), jax.random.fold_in(seeds[2], 1), 0, 1)
    screen_list = draw_screen_list(jax.random.fold_in(seeds[6], 71), 0)
    screen_count = draw_screen_count(jax.random.fold_in(seeds[6], 71), 0)
    owner_order = jax.random.permutation(seeds[5], PAIRS).astype(jnp.int32)
    return {"three_index": three_index, "occ_coeff": occ_coeff, "occ_mask": occ_mask, "screen_list": screen_list, "screen_count": screen_count, "owner_order": owner_order}


def reference(three_index, occ_coeff, occ_mask, screen_list, screen_count, owner_order):
    col_mask = jnp.repeat(occ_mask, OCC_DEV, axis=1).astype(jnp.float32)
    masked_coeff = occ_coeff.astype(jnp.float32).reshape(NBLOCKS, BLOCK, ORBITALS) * col_mask[:, None, :]
    slab = three_index.reshape(NBLOCKS, SLOTS, AUX_ALL, BLOCK, BLOCK)

    def one_aux(carry, aux_index):
        rows = lax.dynamic_slice_in_dim(slab, aux_index * AUX_DEV, AUX_DEV, 2).astype(jnp.float32)
        listed = screen_list[aux_index].reshape(NBLOCKS, SLOTS)
        counts = screen_count[aux_index]
        live = (jnp.arange(SLOTS)[None, :] < counts[:, None]).astype(jnp.float32)
        coeff = masked_coeff[listed] * live[:, :, None, None]
        half = jnp.einsum('msni,msqpn->miqp', coeff, rows, precision=lax.Precision.HIGHEST)
        half = (half * col_mask[:, :, None, None]).astype(jnp.bfloat16)
        flat = half.astype(jnp.float32).reshape(NBLOCKS, ORBITALS * AUX_DEV, BLOCK)
        contrib = jnp.einsum('mrp,nrq->mpnq', flat, flat, precision=lax.Precision.HIGHEST)
        return (carry + contrib, None)
    start = jnp.zeros((NBLOCKS, BLOCK, NBLOCKS, BLOCK), jnp.float32)
    dense, _ = lax.scan(one_aux, start, jnp.arange(N_AUX, dtype=jnp.int32))
    blocks = dense.transpose(0, 2, 1, 3).reshape(PAIRS, BLOCK, BLOCK)
    scale = 1.0 / math.sqrt(AUX_ALL * ORBITALS)
    return blocks[owner_order] * scale
```

```python
import math

import jax
import jax.numpy as jnp
from jax import lax
from jax.experimental import pallas as pl
from jax.experimental.pallas import tpu as pltpu
from jax.sharding import PartitionSpec as P

MESH = pl.DeviceIdType.MESH
NX, NC, NY, NZ = 4, 2, 4, 8
NOCC = NX * NC
BLOCK = 128
SLOTS = 4
ORB = 256
AUX = 64
CHUNK = 16
PHASES = BLOCK // CHUNK
QD = AUX // NOCC
DEPTH = QD * ORB


def kernel(
    three_ref, coeff_ref, mask_ref, list_ref, count_ref, order_ref, out_ref,
    tbuf, cbuf, cm, sbuf, xbuf, hbuf, pack, crecv, yrecv, zrecv, b1, b2, fsend, frecv,
    tsem, csem, xss, xrs, css, crs, yss, yrs, zss, zrs, fss, frs,
):
    occ, aux = lax.axis_index("occ"), lax.axis_index("aux")
    x, c = occ // NC, occ % NC
    y, z = aux // NZ, aux % NZ

    def occ_to(e):
        return ((x + e // 2 + 1) % NX) * NC + (c + e) % NC

    def occ_from(e):
        return ((x + 2 * NX - e // 2 - 1) % NX) * NC + (c + e) % NC

    def at_occ(o):
        return (aux, o)

    def at_y(i):
        return (((y + i + 1) % NY) * NZ + z, occ)

    def at_z(i):
        return (y * NZ + (z + i + 1) % NZ, occ)

    barrier = pltpu.get_barrier_semaphore()
    for e in (0, 1, 2, 3, 4, 5, 7):
        pl.semaphore_signal(barrier, inc=1, device_id=at_occ(occ_to(e)), device_id_type=MESH)
    for i in range(NY - 1):
        pl.semaphore_signal(barrier, inc=1, device_id=at_y(i), device_id_type=MESH)
    for i in range(NZ - 1):
        pl.semaphore_signal(barrier, inc=1, device_id=at_z(i), device_id_type=MESH)

    def rows(t):
        return pl.ds(pl.multiple_of(t * CHUNK, CHUNK), CHUNK)

    def load(t):
        return pltpu.make_async_copy(three_ref.at[:, :, rows(t), :], tbuf.at[t], tsem.at[t])

    def x_copy(e, t):
        return pltpu.make_async_remote_copy(
            src_ref=sbuf.at[e, rows(t)], dst_ref=xbuf.at[occ, rows(t)],
            send_sem=xss.at[e, t], recv_sem=xrs.at[e, t],
            device_id=at_occ(occ_to(e)), device_id_type=MESH,
        )

    def x_arrival(e, t):
        return pltpu.make_async_remote_copy(
            src_ref=sbuf.at[e, rows(t)], dst_ref=xbuf.at[occ_from(e), rows(t)],
            send_sem=xss.at[e, t], recv_sem=xrs.at[e, t],
            device_id=at_occ(occ_to(e)), device_id_type=MESH,
        )

    def c_copy(t):
        return pltpu.make_async_remote_copy(
            src_ref=pack.at[t, 1 - c], dst_ref=crecv.at[t],
            send_sem=css.at[t], recv_sem=crs.at[t],
            device_id=at_occ(occ_to(7)), device_id_type=MESH,
        )

    def y_copy(t, i):
        return pltpu.make_async_remote_copy(
            src_ref=pack.at[t, c, (y + i + 1) % NY], dst_ref=yrecv.at[t, i],
            send_sem=yss.at[t, i], recv_sem=yrs.at[t, i],
            device_id=at_y(i), device_id_type=MESH,
        )

    def z_copy(t, i):
        return pltpu.make_async_remote_copy(
            src_ref=pack.at[t, c, y, (z + i + 1) % NZ], dst_ref=zrecv.at[t, i],
            send_sem=zss.at[t, i], recv_sem=zrs.at[t, i],
            device_id=at_z(i), device_id_type=MESH,
        )

    def loop(n, body):
        def step(i, carry):
            body(i)
            return carry

        lax.fori_loop(0, n, step, 0)

    coeff_copy = pltpu.make_async_copy(coeff_ref, cbuf, csem)
    coeff_copy.start()
    loop(PHASES, lambda t: load(t).start())

    group = lax.broadcasted_iota(jnp.int32, (1, ORB), 1) // (ORB // NOCC)
    hbuf[...] = jnp.zeros_like(hbuf)
    coeff_copy.wait()
    for s in range(SLOTS):
        n = list_ref[0, s]
        live = (s < count_ref[0, 0]).astype(jnp.int32)
        column = jnp.zeros((1, ORB), jnp.int32)
        for o in range(NOCC):
            column = jnp.where(group == o, mask_ref[n, o] * mask_ref[occ, o] * live, column)
        cm[pl.ds(s * BLOCK, BLOCK), :] = (cbuf[n].astype(jnp.float32) * column.astype(jnp.float32)).astype(jnp.bfloat16)

    def half(t, dest, target):
        first = pl.multiple_of(dest * QD, QD)
        left = jnp.concatenate(
            [tbuf[t, s, pl.ds(first, QD)].reshape(QD * CHUNK, BLOCK) for s in range(SLOTS)], axis=1
        )
        value = jnp.dot(left, cm[...], preferred_element_type=jnp.float32).astype(jnp.bfloat16)
        for q in range(QD):
            target[rows(t), pl.ds(q * ORB, ORB)] = value[q * CHUNK : (q + 1) * CHUNK]

    def send(e, t):
        half(t, occ_to(e), sbuf.at[e])
        x_copy(e, t).start()

    load(0).wait()
    half(0, occ_to(0), sbuf.at[0])
    half(0, occ_to(1), sbuf.at[1])
    pl.semaphore_wait(barrier, 7 + NY - 1 + NZ - 1)
    x_copy(0, 0).start()
    x_copy(1, 0).start()
    lax.fori_loop(2, 6, lambda e, v: (send(e, 0), v)[1], 0)
    send(7, 0)
    half(0, occ, xbuf.at[occ])

    def produce(t, carry):
        load(t).wait()
        loop(6, lambda e: send(e, t))
        send(7, t)
        half(t, occ, xbuf.at[occ])
        return carry

    lax.fori_loop(1, PHASES, produce, 0)

    def pair_sums(t):
        width = (t + 1) * CHUNK
        for e in (0, 1, 2, 3, 4, 5, 7):
            x_arrival(e, t).wait_recv()

        def one(n):
            left = xbuf[:, t * CHUNK : (t + 1) * CHUNK, :].reshape(NOCC * CHUNK, DEPTH)
            value = lax.dot_general(
                left, xbuf[n, :width, :], (((1,), (1,)), ((), ())), preferred_element_type=jnp.float32
            )
            hbuf[:, n, :, :width] = value.reshape(NOCC, CHUNK, width)

        loop(NOCC, one)

        def place(a):
            for parity in range(NC):
                o = order_ref[NC * a + parity]
                m, n = o // NOCC, o % NOCC
                pack[t, parity, a // NZ, a % NZ, :CHUNK, :] = hbuf[m, n]
                pack[t, parity, a // NZ, a % NZ, CHUNK:, :] = hbuf[n, m]

        loop(NY * NZ, place)
        c_copy(t).start()

    def after_core(t):
        c_copy(t).wait_recv()

        def one(i):
            pack[t, c, i] = pack[t, c, i] + crecv[t, i]

        loop(NY, one)
        loop(NY - 1, lambda i: y_copy(t, i).start())

    def after_y(t):
        loop(NY - 1, lambda i: y_copy(t, i).wait_recv())
        total = pack[t, c, y]
        for i in range(NY - 1):
            total = total + yrecv[t, i]
        pack[t, c, y] = total
        loop(NZ - 1, lambda i: z_copy(t, i).start())

    def after_z(t):
        loop(NZ - 1, lambda i: z_copy(t, i).wait_recv())
        total = pack[t, c, y, z]
        for i in range(NZ - 1):
            total = total + zrecv[t, i]
        b1[t * CHUNK : (t + 1) * CHUNK, :] = total[:CHUNK]
        b2[t * CHUNK : (t + 1) * CHUNK, :] = total[CHUNK:]

    for t in range(PHASES + 2):
        if t < PHASES:
            pair_sums(t)
        if t >= 2:
            after_z(t - 2)
        if 1 <= t <= PHASES:
            after_y(t - 1)
        if t < PHASES:
            after_core(t)

    p = lax.broadcasted_iota(jnp.int32, (BLOCK, BLOCK), 0)
    q = lax.broadcasted_iota(jnp.int32, (BLOCK, BLOCK), 1)
    whole = jnp.where(q < (p // CHUNK + 1) * CHUNK, b1[...], b2[...].T)
    fsend[...] = whole.reshape(NOCC, CHUNK, BLOCK)

    def f_copy(e):
        return pltpu.make_async_remote_copy(
            src_ref=fsend.at[occ_to(e)], dst_ref=frecv.at[occ],
            send_sem=fss.at[e], recv_sem=frs.at[e],
            device_id=at_occ(occ_to(e)), device_id_type=MESH,
        )

    for e in (0, 1, 2, 3, 4, 5, 7):
        f_copy(e).start()
    frecv[occ] = fsend[occ]

    def drain(t):
        loop(6, lambda e: x_copy(e, t).wait_send())
        x_copy(7, t).wait_send()
        c_copy(t).wait_send()
        loop(NY - 1, lambda i: y_copy(t, i).wait_send())
        loop(NZ - 1, lambda i: z_copy(t, i).wait_send())

    loop(PHASES, drain)
    for e in (0, 1, 2, 3, 4, 5, 7):
        f_copy(e).wait()
    scale = 1.0 / math.sqrt(AUX * NY * NZ * ORB)
    for parity in range(NC):
        total = frecv[parity]
        for i in range(1, NX):
            total = total + frecv[NC * i + parity]
        out_ref[parity] = total * scale


def shards(three_index, occ_coeff, occ_mask, screen_list, screen_count, owner_order):
    f32, bf16, dma = jnp.float32, jnp.bfloat16, pltpu.SemaphoreType.DMA
    smem = pl.BlockSpec(memory_space=pltpu.SMEM)
    anywhere = pl.BlockSpec(memory_space=pl.ANY)
    return pl.pallas_call(
        kernel,
        out_shape=jax.ShapeDtypeStruct((NC, CHUNK, BLOCK), f32),
        in_specs=[anywhere, anywhere, smem, smem, smem, smem],
        out_specs=pl.BlockSpec(memory_space=pltpu.VMEM),
        scratch_shapes=[
            pltpu.VMEM((PHASES, SLOTS, AUX, CHUNK, BLOCK), bf16),
            pltpu.VMEM((NOCC, BLOCK, ORB), bf16),
            pltpu.VMEM((SLOTS * BLOCK, ORB), bf16),
            pltpu.VMEM((NOCC, BLOCK, DEPTH), bf16),
            pltpu.VMEM((NOCC, BLOCK, DEPTH), bf16),
            pltpu.VMEM((NOCC, NOCC, CHUNK, BLOCK), f32),
            pltpu.VMEM((PHASES, NC, NY, NZ, 2 * CHUNK, BLOCK), f32),
            pltpu.VMEM((PHASES, NY, NZ, 2 * CHUNK, BLOCK), f32),
            pltpu.VMEM((PHASES, NY - 1, NZ, 2 * CHUNK, BLOCK), f32),
            pltpu.VMEM((PHASES, NZ - 1, 2 * CHUNK, BLOCK), f32),
            pltpu.VMEM((BLOCK, BLOCK), f32),
            pltpu.VMEM((BLOCK, BLOCK), f32),
            pltpu.VMEM((NOCC, CHUNK, BLOCK), f32),
            pltpu.VMEM((NOCC, CHUNK, BLOCK), f32),
            dma((PHASES,)),
            dma,
            dma((8, PHASES)),
            dma((8, PHASES)),
            dma((PHASES,)),
            dma((PHASES,)),
            dma((PHASES, NY - 1)),
            dma((PHASES, NY - 1)),
            dma((PHASES, NZ - 1)),
            dma((PHASES, NZ - 1)),
            dma((8,)),
            dma((8,)),
        ],
        compiler_params=pltpu.CompilerParams(
            collective_id=0, has_side_effects=True, vmem_limit_bytes=56 * 1024 * 1024
        ),
        name="exchange",
    )(three_index, occ_coeff.reshape(NOCC, BLOCK, ORB), occ_mask, screen_list, screen_count, owner_order)


def solution(mesh):
    in_specs = (P("occ", "aux", None, None), P(), P(), P("aux", "occ"), P("aux", "occ"), P())
    out_specs = P("aux", "occ", None)
    return jax.shard_map(shards, mesh=mesh, in_specs=in_specs, out_specs=out_specs, check_vma=False)
```

```python
import math

import jax
import jax.numpy as jnp
from jax import lax
from jax.experimental import pallas as pl
from jax.experimental.pallas import tpu as pltpu
from jax.sharding import PartitionSpec as P

MESH = pl.DeviceIdType.MESH
NX, NC, NY, NZ = 4, 2, 4, 8
NOCC = NX * NC
BLOCK = 128
SLOTS = 4
ORB = 256
AUX = 64
CHUNK = 16
PHASES = BLOCK // CHUNK
QD = AUX // NOCC
DEPTH = QD * ORB
STEPS = ((2, 0), (2, 1), (1, 0), (3, 0), (1, 1), (3, 1), (0, 1))
PARTNERS = range(len(STEPS))
MATE = len(STEPS) - 1
HALF = PHASES // 2


def kernel(
    three_ref, coeff_ref, mask_ref, list_ref, count_ref, order_ref, out_ref,
    tbuf, cbuf, cm, sbuf, xbuf, wbuf, rbuf, hbuf, early, early_c, early_y, early_z, late, late_c, late_y, late_z, b1, b2, fsend, frecv,
    tsem, csem, xss, xrs, css, crs, yss, yrs, zss, zrs, fss, frs,
):
    occ, aux = lax.axis_index("occ"), lax.axis_index("aux")
    x, c = occ // NC, occ % NC
    y, z = aux // NZ, aux % NZ

    def occ_to(e):
        return ((x + STEPS[e][0]) % NX) * NC + (c + STEPS[e][1]) % NC

    def occ_from(e):
        return ((x + NX - STEPS[e][0]) % NX) * NC + (c + STEPS[e][1]) % NC

    def at_occ(o):
        return (aux, o)

    def at_y(i):
        return (((y + i + 1) % NY) * NZ + z, occ)

    def at_z(i):
        return (y * NZ + (z + i + 1) % NZ, occ)

    barrier = pltpu.get_barrier_semaphore()
    for e in PARTNERS:
        pl.semaphore_signal(barrier, inc=1, device_id=at_occ(occ_to(e)), device_id_type=MESH)
    for i in range(NY - 1):
        pl.semaphore_signal(barrier, inc=1, device_id=at_y(i), device_id_type=MESH)
    for i in range(NZ - 1):
        pl.semaphore_signal(barrier, inc=1, device_id=at_z(i), device_id_type=MESH)

    def rows(t):
        return pl.ds(pl.multiple_of(t * CHUNK, CHUNK), CHUNK)

    def load(t):
        return pltpu.make_async_copy(three_ref.at[:, :, rows(t), :], tbuf.at[t], tsem.at[t])

    def x_copy(e, t):
        return pltpu.make_async_remote_copy(
            src_ref=sbuf.at[e, rows(t)], dst_ref=xbuf.at[occ, rows(t)],
            send_sem=xss.at[e, t], recv_sem=xrs.at[e, t],
            device_id=at_occ(occ_to(e)), device_id_type=MESH,
        )

    def x_arrival(e, t):
        return pltpu.make_async_remote_copy(
            src_ref=sbuf.at[e, rows(t)], dst_ref=xbuf.at[occ_from(e), rows(t)],
            send_sem=xss.at[e, t], recv_sem=xrs.at[e, t],
            device_id=at_occ(occ_to(e)), device_id_type=MESH,
        )

    def packs(t):
        if t < HALF:
            return early.at[t], early_c.at[t], early_y.at[t], early_z.at[t]
        return late.at[t - HALF], late_c.at[t - HALF], late_y.at[t - HALF], late_z.at[t - HALF]

    def c_copy(t):
        pack, crecv, _, _ = packs(t)
        return pltpu.make_async_remote_copy(
            src_ref=pack.at[1 - c], dst_ref=crecv,
            send_sem=css.at[t], recv_sem=crs.at[t],
            device_id=at_occ(occ_to(MATE)), device_id_type=MESH,
        )

    def y_copy(t, i):
        pack, _, yrecv, _ = packs(t)
        return pltpu.make_async_remote_copy(
            src_ref=pack.at[c, (y + i + 1) % NY], dst_ref=yrecv.at[i],
            send_sem=yss.at[t, i], recv_sem=yrs.at[t, i],
            device_id=at_y(i), device_id_type=MESH,
        )

    def z_copy(t, i):
        pack, _, _, zrecv = packs(t)
        return pltpu.make_async_remote_copy(
            src_ref=pack.at[c, y, (z + i + 1) % NZ], dst_ref=zrecv.at[i],
            send_sem=zss.at[t, i], recv_sem=zrs.at[t, i],
            device_id=at_z(i), device_id_type=MESH,
        )

    def loop(n, body):
        def step(i, carry):
            body(i)
            return carry

        lax.fori_loop(0, n, step, 0)

    coeff_copy = pltpu.make_async_copy(coeff_ref, cbuf, csem)
    coeff_copy.start()
    loop(PHASES, lambda t: load(t).start())

    group = lax.broadcasted_iota(jnp.int32, (1, ORB), 1) // (ORB // NOCC)
    coeff_copy.wait()
    for s in range(SLOTS):
        n = list_ref[0, s]
        live = (s < count_ref[0, 0]).astype(jnp.int32)
        column = jnp.zeros((1, ORB), jnp.int32)
        for o in range(NOCC):
            column = jnp.where(group == o, mask_ref[n, o] * mask_ref[occ, o] * live, column)
        cm[pl.ds(s * BLOCK, BLOCK), :] = (cbuf[n].astype(jnp.float32) * column.astype(jnp.float32)).astype(jnp.bfloat16)

    def half(t, dest, target):
        first = pl.multiple_of(dest * QD, QD)
        left = jnp.concatenate(
            [tbuf[t, s, pl.ds(first, QD)].reshape(QD * CHUNK, BLOCK) for s in range(SLOTS)], axis=1
        )
        value = jnp.dot(left, cm[...], preferred_element_type=jnp.float32).astype(jnp.bfloat16)
        for q in range(QD):
            target[rows(t), pl.ds(q * ORB, ORB)] = value[q * CHUNK : (q + 1) * CHUNK]

    def send(e, t):
        half(t, occ_to(e), sbuf.at[e])
        x_copy(e, t).start()

    load(0).wait()
    for e in range(4):
        half(0, occ_to(e), sbuf.at[e])
    pl.semaphore_wait(barrier, len(STEPS) + NY - 1 + NZ - 1)
    for e in range(4):
        x_copy(e, 0).start()
    for e in PARTNERS[4:]:
        send(e, 0)
    half(0, occ, xbuf.at[occ])

    def produce(t, carry):
        load(t).wait()
        for e in PARTNERS:
            send(e, t)
        half(t, occ, xbuf.at[occ])
        return carry

    lax.fori_loop(1, PHASES, produce, 0)

    def pair_sums(t):
        for e in PARTNERS:
            x_arrival(e, t).wait_recv()
        left = xbuf[:, t * CHUNK : (t + 1) * CHUNK, :].reshape(BLOCK, DEPTH)

        for i in range(QD):
            wbuf[t // 2, i * ORB : (i + 1) * ORB, t % 2 * BLOCK : (t % 2 + 1) * BLOCK] = left[:, i * ORB : (i + 1) * ORB].T

        def product(u):
            value = jnp.dot(left, wbuf[u], preferred_element_type=jnp.float32)
            rbuf[2 * u] = value[:, :BLOCK].reshape(NOCC, CHUNK, BLOCK)
            rbuf[2 * u + 1] = value[:, BLOCK:].reshape(NOCC, CHUNK, BLOCK)

        loop(t // 2 + 1, product)

        if t >= 2:
            after_y(t - 2)

        segment = lax.broadcasted_iota(jnp.int32, (CHUNK, BLOCK), 1) // CHUNK

        for d in (1, 2, 4):
            low = segment & d == 0
            for m in range(NOCC):
                for i in range(PHASES):
                    if i & d == 0:
                        one, two = rbuf[i, m], rbuf[i + d, m]
                        first = jnp.where(low, one, pltpu.roll(two, d * CHUNK, 1))
                        second = jnp.where(low, pltpu.roll(one, BLOCK - d * CHUNK, 1), two)
                        if d < 4:
                            rbuf[i, m], rbuf[i + d, m] = first, second
                        else:
                            hbuf[m, i], hbuf[m, i + d] = first, second

        def place(g):
            for k in range(NC * NZ // 2):
                a, parity = g * (NZ // 2) + k // NC, k % NC
                o = order_ref[NC * a + parity]
                m, n = o >> 3, o & 7
                if t < HALF:
                    turned = pltpu.roll(hbuf[n, m], BLOCK // 2, 1)
                    early[t, parity, a // NZ, a % NZ] = jnp.where(segment < HALF, hbuf[m, n], turned)
                else:
                    late[t - HALF, parity, a // NZ, a % NZ, :CHUNK] = hbuf[m, n]
                    late[t - HALF, parity, a // NZ, a % NZ, CHUNK:] = hbuf[n, m]

        loop(2 * NY, place)
        c_copy(t).start()

    def after_core(t):
        pack, crecv, _, _ = packs(t)
        c_copy(t).wait_recv()

        def one(i):
            pack[c, i] = pack[c, i] + crecv[i]

        loop(NY, one)
        loop(NY - 1, lambda i: y_copy(t, i).start())

    def after_y(t):
        pack, _, yrecv, _ = packs(t)
        loop(NY - 1, lambda i: y_copy(t, i).wait_recv())
        total = pack[c, y]
        for i in range(NY - 1):
            total = total + yrecv[i]
        pack[c, y] = total
        loop(NZ - 1, lambda i: z_copy(t, i).start())

    def after_z(t):
        pack, _, _, zrecv = packs(t)
        loop(NZ - 1, lambda i: z_copy(t, i).wait_recv())
        total = pack[c, y, z]
        for i in range(NZ - 1):
            total = total + zrecv[i]
        b1[t * CHUNK : (t + 1) * CHUNK, :] = total[:CHUNK]
        b2[t * CHUNK : (t + 1) * CHUNK, :] = pltpu.roll(total, BLOCK // 2, 1) if t < HALF else total[CHUNK:]

    for t in range(PHASES):
        pair_sums(t)
        if t >= 3:
            after_z(t - 3)
        after_core(t)
    after_y(PHASES - 2)
    after_z(PHASES - 3)
    after_y(PHASES - 1)
    after_z(PHASES - 2)
    after_z(PHASES - 1)

    p = lax.broadcasted_iota(jnp.int32, (BLOCK, BLOCK), 0)
    q = lax.broadcasted_iota(jnp.int32, (BLOCK, BLOCK), 1)
    whole = jnp.where(q < (p // CHUNK + 1) * CHUNK, b1[...], b2[...].T)
    fsend[...] = whole.reshape(NOCC, CHUNK, BLOCK)

    def f_copy(e):
        return pltpu.make_async_remote_copy(
            src_ref=fsend.at[occ_to(e)], dst_ref=frecv.at[occ],
            send_sem=fss.at[e], recv_sem=frs.at[e],
            device_id=at_occ(occ_to(e)), device_id_type=MESH,
        )

    for e in PARTNERS:
        f_copy(e).start()
    frecv[occ] = fsend[occ]

    for t in range(PHASES):
        for e in PARTNERS:
            x_copy(e, t).wait_send()
        c_copy(t).wait_send()
        loop(NY - 1, lambda i: y_copy(t, i).wait_send())
        loop(NZ - 1, lambda i: z_copy(t, i).wait_send())
    for e in PARTNERS:
        f_copy(e).wait()
    scale = 1.0 / math.sqrt(AUX * NY * NZ * ORB)
    for parity in range(NC):
        total = frecv[parity]
        for i in range(1, NX):
            total = total + frecv[NC * i + parity]
        out_ref[parity] = total * scale


def shards(three_index, occ_coeff, occ_mask, screen_list, screen_count, owner_order):
    f32, bf16, dma = jnp.float32, jnp.bfloat16, pltpu.SemaphoreType.DMA
    smem = pl.BlockSpec(memory_space=pltpu.SMEM)
    anywhere = pl.BlockSpec(memory_space=pl.ANY)
    return pl.pallas_call(
        kernel,
        out_shape=jax.ShapeDtypeStruct((NC, CHUNK, BLOCK), f32),
        in_specs=[anywhere, anywhere, smem, smem, smem, smem],
        out_specs=pl.BlockSpec(memory_space=pltpu.VMEM),
        scratch_shapes=[
            pltpu.VMEM((PHASES, SLOTS, AUX, CHUNK, BLOCK), bf16),
            pltpu.VMEM((NOCC, BLOCK, ORB), bf16),
            pltpu.VMEM((SLOTS * BLOCK, ORB), bf16),
            pltpu.VMEM((len(STEPS), BLOCK, DEPTH), bf16),
            pltpu.VMEM((NOCC, BLOCK, DEPTH), bf16),
            pltpu.VMEM((PHASES // 2, DEPTH, 2 * BLOCK), bf16),
            pltpu.VMEM((PHASES, NOCC, CHUNK, BLOCK), f32),
            pltpu.VMEM((NOCC, NOCC, CHUNK, BLOCK), f32),
            *(
                pltpu.VMEM((HALF, *lead, height, BLOCK), f32)
                for height in (CHUNK, 2 * CHUNK)
                for lead in ((NC, NY, NZ), (NY, NZ), (NY - 1, NZ), (NZ - 1,))
            ),
            pltpu.VMEM((BLOCK, BLOCK), f32),
            pltpu.VMEM((BLOCK, BLOCK), f32),
            pltpu.VMEM((NOCC, CHUNK, BLOCK), f32),
            pltpu.VMEM((NOCC, CHUNK, BLOCK), f32),
            dma((PHASES,)),
            dma,
            dma((len(STEPS), PHASES)),
            dma((len(STEPS), PHASES)),
            dma((PHASES,)),
            dma((PHASES,)),
            dma((PHASES, NY - 1)),
            dma((PHASES, NY - 1)),
            dma((PHASES, NZ - 1)),
            dma((PHASES, NZ - 1)),
            dma((len(STEPS),)),
            dma((len(STEPS),)),
        ],
        compiler_params=pltpu.CompilerParams(
            collective_id=0, has_side_effects=True, vmem_limit_bytes=56 * 1024 * 1024
        ),
        name="exchange",
    )(three_index, occ_coeff.reshape(NOCC, BLOCK, ORB), occ_mask, screen_list, screen_count, owner_order)


def solution(mesh):
    in_specs = (P("occ", "aux", None, None), P(), P(), P("aux", "occ"), P("aux", "occ"), P())
    out_specs = P("aux", "occ", None)
    return jax.shard_map(shards, mesh=mesh, in_specs=in_specs, out_specs=out_specs, check_vma=False)
```

```python
import math

import jax
import jax.numpy as jnp
from jax import lax
from jax.experimental import pallas as pl
from jax.experimental.pallas import tpu as pltpu
from jax.sharding import PartitionSpec as P

MESH = pl.DeviceIdType.MESH
NX, NC, NY, NZ = 4, 2, 4, 8
NOCC = NX * NC
BLOCK = 128
SLOTS = 4
ORB = 256
AUX = 64
CHUNK = 16
SUB = CHUNK // 2
CHUNKS = BLOCK // CHUNK
FULL = CHUNKS - 1
PHASES = FULL + 2
QD = AUX // NOCC
DEPTH = QD * ORB
START = (*range(0, BLOCK - CHUNK + 1, CHUNK), BLOCK - SUB, BLOCK)
Y_STEPS = (2, 1, 3)
Z_STEPS = (4, 3, 5, 2, 6, 1, 7)
STEPS = ((2, 0), (2, 1), (1, 0), (3, 0), (1, 1), (3, 1), (0, 1))
PARTNERS = range(len(STEPS))
MATE = len(STEPS) - 1
HALF = CHUNKS // 2


def kernel(
    three_ref, coeff_ref, mask_ref, list_ref, count_ref, order_ref, out_ref,
    tbuf, cbuf, cm, sbuf, xbuf, ssub, xsub, wbuf, wsub, rbuf, hbuf, early, early_c, early_y, early_z, late, late_c, late_y, late_z, last, last_c, last_y, last_z, b1, b2, fsend, frecv,
    tsem, fsem, csem, xss, xrs, css, crs, yss, yrs, zss, zrs, fss, frs,
):
    occ, aux = lax.axis_index("occ"), lax.axis_index("aux")
    x, c = occ // NC, occ % NC
    y, z = aux // NZ, aux % NZ

    def occ_to(e):
        return ((x + STEPS[e][0]) % NX) * NC + (c + STEPS[e][1]) % NC

    def occ_from(e):
        return ((x + NX - STEPS[e][0]) % NX) * NC + (c + STEPS[e][1]) % NC

    def at_occ(o):
        return (aux, o)

    def at_y(i):
        return (((y + Y_STEPS[i]) % NY) * NZ + z, occ)

    def at_z(i):
        return (y * NZ + (z + Z_STEPS[i]) % NZ, occ)

    barrier = pltpu.get_barrier_semaphore()
    for e in PARTNERS:
        pl.semaphore_signal(barrier, inc=1, device_id=at_occ(occ_to(e)), device_id_type=MESH)
    for i in range(NY - 1):
        pl.semaphore_signal(barrier, inc=1, device_id=at_y(i), device_id_type=MESH)
    for i in range(NZ - 1):
        pl.semaphore_signal(barrier, inc=1, device_id=at_z(i), device_id_type=MESH)

    def rows(t):
        return pl.ds(pl.multiple_of(t * CHUNK, CHUNK), CHUNK)

    def load(t):
        return pltpu.make_async_copy(three_ref.at[:, :, rows(t), :], tbuf.at[t], tsem.at[t])

    def load_first(d):
        at = pl.ds(pl.multiple_of(d * QD, QD), QD)
        return pltpu.make_async_copy(three_ref.at[:, at, :CHUNK, :], tbuf.at[0, :, at], fsem.at[d])

    def x_ends(e, t, sender):
        if isinstance(t, int) and t >= FULL:
            return ssub.at[e, t - FULL], xsub.at[t - FULL, sender]
        return sbuf.at[e, rows(t)], xbuf.at[sender, rows(t)]

    def x_copy(e, t):
        source, target = x_ends(e, t, occ)
        return pltpu.make_async_remote_copy(
            src_ref=source, dst_ref=target,
            send_sem=xss.at[e, t], recv_sem=xrs.at[e, t],
            device_id=at_occ(occ_to(e)), device_id_type=MESH,
        )

    def x_arrival(e, t):
        source, target = x_ends(e, t, occ_from(e))
        return pltpu.make_async_remote_copy(
            src_ref=source, dst_ref=target,
            send_sem=xss.at[e, t], recv_sem=xrs.at[e, t],
            device_id=at_occ(occ_to(e)), device_id_type=MESH,
        )

    def packs(t):
        if t < HALF:
            return early.at[t], early_c.at[t], early_y.at[t], early_z.at[t]
        if t < FULL:
            return late.at[t - HALF], late_c.at[t - HALF], late_y.at[t - HALF], late_z.at[t - HALF]
        return last.at[t - FULL], last_c.at[t - FULL], last_y.at[t - FULL], last_z.at[t - FULL]

    def group_of(i):
        return (y + Y_STEPS[i]) % NY if i < NY - 1 else y

    def c_copy(t, i):
        pack, crecv, _, _ = packs(t)
        at = group_of(i)
        return pltpu.make_async_remote_copy(
            src_ref=pack.at[1 - c, at], dst_ref=crecv.at[at],
            send_sem=css.at[t, i], recv_sem=crs.at[t, i],
            device_id=at_occ(occ_to(MATE)), device_id_type=MESH,
        )

    def y_copy(t, i):
        pack, _, yrecv, _ = packs(t)
        return pltpu.make_async_remote_copy(
            src_ref=pack.at[c, group_of(i)], dst_ref=yrecv.at[i],
            send_sem=yss.at[t, i], recv_sem=yrs.at[t, i],
            device_id=at_y(i), device_id_type=MESH,
        )

    def z_copy(t, i):
        pack, _, _, zrecv = packs(t)
        return pltpu.make_async_remote_copy(
            src_ref=pack.at[c, y, (z + Z_STEPS[i]) % NZ], dst_ref=zrecv.at[i],
            send_sem=zss.at[t, i], recv_sem=zrs.at[t, i],
            device_id=at_z(i), device_id_type=MESH,
        )

    def loop(n, body):
        def step(i, carry):
            body(i)
            return carry

        lax.fori_loop(0, n, step, 0)

    coeff_copy = pltpu.make_async_copy(coeff_ref, cbuf, csem)
    coeff_copy.start()
    for e in PARTNERS:
        load_first(occ_to(e)).start()
    load_first(occ).start()

    group = lax.broadcasted_iota(jnp.int32, (1, ORB), 1) // (ORB // NOCC)
    coeff_copy.wait()
    for s in range(SLOTS):
        n = list_ref[0, s]
        live = (s < count_ref[0, 0]).astype(jnp.int32)
        column = jnp.zeros((1, ORB), jnp.int32)
        for o in range(NOCC):
            column = jnp.where(group == o, mask_ref[n, o] * mask_ref[occ, o] * live, column)
        cm[pl.ds(s * BLOCK, BLOCK), :] = (cbuf[n].astype(jnp.float32) * column.astype(jnp.float32)).astype(jnp.bfloat16)

    def half_rows(t, dest):
        first = pl.multiple_of(dest * QD, QD)
        left = jnp.concatenate(
            [tbuf[t, s, pl.ds(first, QD)].reshape(QD * CHUNK, BLOCK) for s in range(SLOTS)], axis=1
        )
        return jnp.dot(left, cm[...], preferred_element_type=jnp.float32)

    def half(t, dest, target):
        value = half_rows(t, dest).astype(jnp.bfloat16)
        for q in range(QD):
            target[rows(t), pl.ds(q * ORB, ORB)] = value[q * CHUNK : (q + 1) * CHUNK]

    def half_last(dest, targets):
        value = half_rows(FULL, dest).reshape(QD, 2, SUB, ORB)
        for s, target in enumerate(targets):
            for q in range(QD // 2):
                pair = jnp.concatenate([value[q, s], value[q + QD // 2, s]], axis=0)
                target[:, q * ORB : (q + 1) * ORB] = pair.astype(jnp.bfloat16)

    def send(e, t):
        half(t, occ_to(e), sbuf.at[e])
        x_copy(e, t).start()

    for e in PARTNERS:
        load_first(occ_to(e)).wait()
        half(0, occ_to(e), sbuf.at[e])
        if e == 3:
            lax.fori_loop(1, CHUNKS, lambda t, v: (load(t).start(), v)[1], 0)
            pl.semaphore_wait(barrier, len(STEPS) + NY - 1 + NZ - 1)
            for i in range(e):
                x_copy(i, 0).start()
        if e >= 3:
            x_copy(e, 0).start()
    load_first(occ).wait()
    half(0, occ, xbuf.at[occ])

    def produce(t, carry):
        load(t).wait()
        for e in PARTNERS:
            send(e, t)
        half(t, occ, xbuf.at[occ])
        return carry

    lax.fori_loop(1, FULL, produce, 0)
    load(FULL).wait()
    for e in PARTNERS:
        half_last(occ_to(e), (ssub.at[e, 0], ssub.at[e, 1]))
        x_copy(e, FULL).start()
    for e in PARTNERS:
        x_copy(e, FULL + 1).start()
    half_last(occ, (xsub.at[0, occ], xsub.at[1, occ]))

    def pair_sums(t):
        for e in PARTNERS:
            x_arrival(e, t).wait_recv()
        height = START[t + 1] - START[t]
        if t < FULL:
            left = xbuf[:, t * CHUNK : (t + 1) * CHUNK, :].reshape(BLOCK, DEPTH)
            for i in range(QD):
                wbuf[t // 2, i * ORB : (i + 1) * ORB, t % 2 * BLOCK : (t % 2 + 1) * BLOCK] = left[:, i * ORB : (i + 1) * ORB].T
            for u in range(t // 2 + 1):
                value = jnp.dot(left, wbuf[u], preferred_element_type=jnp.float32)
                rbuf[2 * u] = value[:, :BLOCK].reshape(NOCC, CHUNK, BLOCK)
                rbuf[2 * u + 1] = value[:, BLOCK:].reshape(NOCC, CHUNK, BLOCK)
        else:
            left = xsub[t - FULL].reshape(BLOCK, DEPTH // 2)
            for i in range(QD // 2):
                wsub[t - FULL, i * ORB : (i + 1) * ORB, :] = left[:, i * ORB : (i + 1) * ORB].T

            def halves(value):
                value = value.reshape(NOCC, 2, SUB, value.shape[1])
                return value[:, 0], value[:, 1]

            for u in range(CHUNKS // 2):
                wide = slice(0, 2 * BLOCK if 2 * u + 1 < FULL else BLOCK)
                low = jnp.dot(left, wbuf[u, : DEPTH // 2, wide], preferred_element_type=jnp.float32)
                high = jnp.dot(left, wbuf[u, DEPTH // 2 :, wide], preferred_element_type=jnp.float32)
                value = halves(low)[0] + halves(high)[1]
                rbuf[2 * u, :, :SUB] = value[:, :, :BLOCK]
                if 2 * u + 1 < FULL:
                    rbuf[2 * u + 1, :, :SUB] = value[:, :, BLOCK:]
            low, high = halves(jnp.dot(left, wsub[0], preferred_element_type=jnp.float32))
            value = low + pltpu.roll(high, BLOCK - SUB, 2)
            if t > FULL:
                low, high = halves(jnp.dot(left, wsub[1], preferred_element_type=jnp.float32))
                lane = lax.broadcasted_iota(jnp.int32, (NOCC, SUB, BLOCK), 2)
                value = jnp.where(lane % CHUNK < SUB, value, pltpu.roll(low, SUB, 2) + high)
            rbuf[FULL, :, :SUB] = value

        if 2 <= t < PHASES - 1:
            after_y(t - 2)

        segment = lax.broadcasted_iota(jnp.int32, (height, BLOCK), 1) // CHUNK

        for d in (1, 2, 4):
            low = segment & d == 0
            for m in range(NOCC):
                for i in range(CHUNKS):
                    if i & d == 0:
                        one, two = rbuf[i, m, :height], rbuf[i + d, m, :height]
                        first = jnp.where(low, one, pltpu.roll(two, d * CHUNK, 1))
                        second = jnp.where(low, pltpu.roll(one, BLOCK - d * CHUNK, 1), two)
                        if d < 4:
                            rbuf[i, m, :height], rbuf[i + d, m, :height] = first, second
                        else:
                            hbuf[m, i, :height], hbuf[m, i + d, :height] = first, second

        pack = packs(t)[0]
        for i in range(NY):
            group = group_of(i)
            for k in range(NC * NZ):
                at, parity = k // NC, k % NC
                o = order_ref[NC * NZ * group + k]
                m, n = o >> 3, o & 7
                if t < HALF:
                    turned = pltpu.roll(hbuf[n, m], BLOCK // 2, 1)
                    pack[parity, group, at] = jnp.where(segment < HALF, hbuf[m, n], turned)
                else:
                    pack[parity, group, at, :height] = hbuf[m, n, :height]
                    pack[parity, group, at, height:] = hbuf[n, m, :height]
            c_copy(t, i).start()

    def after_core(t):
        pack, crecv, _, _ = packs(t)
        for i in range(NY):
            at = group_of(i)
            c_copy(t, i).wait_recv()
            pack[c, at] = pack[c, at] + crecv[at]
            if i < NY - 1:
                y_copy(t, i).start()

    def after_y(t):
        pack, _, yrecv, _ = packs(t)
        for i in range(NY - 1):
            y_copy(t, i).wait_recv()
        total = pack[c, y]
        for i in range(NY - 1):
            total = total + yrecv[i]
        pack[c, y] = total
        for i in range(NZ - 1):
            z_copy(t, i).start()

    def after_z(t):
        pack, _, _, zrecv = packs(t)
        for i in range(NZ - 1):
            z_copy(t, i).wait_recv()
        total = pack[c, y, z]
        for i in range(NZ - 1):
            total = total + zrecv[i]
        height = START[t + 1] - START[t]
        b1[START[t] : START[t + 1], :] = total[:height]
        b2[START[t] : START[t + 1], :] = pltpu.roll(total, BLOCK // 2, 1) if t < HALF else total[height:]

    def sent(t):
        for e in PARTNERS:
            x_copy(e, t).wait_send()
        for i in range(NY):
            c_copy(t, i).wait_send()
        for i in range(NY - 1):
            y_copy(t, i).wait_send()
        for i in range(NZ - 1):
            z_copy(t, i).wait_send()

    for t in range(PHASES):
        pair_sums(t)
        if 3 <= t < PHASES - 1:
            after_z(t - 3)
        after_core(t)
        if 3 <= t < PHASES - 1:
            sent(t - 3)
    after_y(PHASES - 3)
    after_z(PHASES - 4)
    after_y(PHASES - 2)
    sent(PHASES - 4)
    after_y(PHASES - 1)
    after_z(PHASES - 3)
    sent(PHASES - 3)
    after_z(PHASES - 2)
    sent(PHASES - 2)
    after_z(PHASES - 1)

    p = lax.broadcasted_iota(jnp.int32, (BLOCK, BLOCK), 0)
    q = lax.broadcasted_iota(jnp.int32, (BLOCK, BLOCK), 1)
    own_end = jnp.where(p < START[FULL], (p // CHUNK + 1) * CHUNK, (p // SUB + 1) * SUB)
    whole = jnp.where(q < own_end, b1[...], b2[...].T)
    fsend[...] = whole.reshape(NOCC, CHUNK, BLOCK)

    def f_copy(e):
        return pltpu.make_async_remote_copy(
            src_ref=fsend.at[occ_to(e)], dst_ref=frecv.at[occ],
            send_sem=fss.at[e], recv_sem=frs.at[e],
            device_id=at_occ(occ_to(e)), device_id_type=MESH,
        )

    for e in PARTNERS:
        f_copy(e).start()
    frecv[occ] = fsend[occ]

    sent(PHASES - 1)
    for e in PARTNERS:
        f_copy(e).wait()
    scale = 1.0 / math.sqrt(AUX * NY * NZ * ORB)
    for parity in range(NC):
        total = frecv[parity]
        for i in range(1, NX):
            total = total + frecv[NC * i + parity]
        out_ref[parity] = total * scale


def shards(three_index, occ_coeff, occ_mask, screen_list, screen_count, owner_order):
    f32, bf16, dma = jnp.float32, jnp.bfloat16, pltpu.SemaphoreType.DMA
    smem = pl.BlockSpec(memory_space=pltpu.SMEM)
    anywhere = pl.BlockSpec(memory_space=pl.ANY)
    return pl.pallas_call(
        kernel,
        out_shape=jax.ShapeDtypeStruct((NC, CHUNK, BLOCK), f32),
        in_specs=[anywhere, anywhere, smem, smem, smem, smem],
        out_specs=pl.BlockSpec(memory_space=pltpu.VMEM),
        scratch_shapes=[
            pltpu.VMEM((CHUNKS, SLOTS, AUX, CHUNK, BLOCK), bf16),
            pltpu.VMEM((NOCC, BLOCK, ORB), bf16),
            pltpu.VMEM((SLOTS * BLOCK, ORB), bf16),
            pltpu.VMEM((len(STEPS), BLOCK, DEPTH), bf16),
            pltpu.VMEM((NOCC, BLOCK, DEPTH), bf16),
            pltpu.VMEM((len(STEPS), 2, CHUNK, DEPTH // 2), bf16),
            pltpu.VMEM((2, NOCC, CHUNK, DEPTH // 2), bf16),
            pltpu.VMEM((CHUNKS // 2, DEPTH, 2 * BLOCK), bf16),
            pltpu.VMEM((2, DEPTH // 2, BLOCK), bf16),
            pltpu.VMEM((CHUNKS, NOCC, CHUNK, BLOCK), f32),
            pltpu.VMEM((NOCC, NOCC, CHUNK, BLOCK), f32),
            *(
                pltpu.VMEM((count, *lead, height, BLOCK), f32)
                for count, height in ((HALF, CHUNK), (FULL - HALF, 2 * CHUNK), (2, CHUNK))
                for lead in ((NC, NY, NZ), (NY, NZ), (NY - 1, NZ), (NZ - 1,))
            ),
            pltpu.VMEM((BLOCK, BLOCK), f32),
            pltpu.VMEM((BLOCK, BLOCK), f32),
            pltpu.VMEM((NOCC, CHUNK, BLOCK), f32),
            pltpu.VMEM((NOCC, CHUNK, BLOCK), f32),
            dma((CHUNKS,)),
            dma((NOCC,)),
            dma,
            dma((len(STEPS), PHASES)),
            dma((len(STEPS), PHASES)),
            dma((PHASES, NY)),
            dma((PHASES, NY)),
            dma((PHASES, NY - 1)),
            dma((PHASES, NY - 1)),
            dma((PHASES, NZ - 1)),
            dma((PHASES, NZ - 1)),
            dma((len(STEPS),)),
            dma((len(STEPS),)),
        ],
        compiler_params=pltpu.CompilerParams(
            collective_id=0, has_side_effects=True, vmem_limit_bytes=56 * 1024 * 1024
        ),
        name="exchange",
    )(three_index, occ_coeff.reshape(NOCC, BLOCK, ORB), occ_mask, screen_list, screen_count, owner_order)


def solution(mesh):
    in_specs = (P("occ", "aux", None, None), P(), P(), P("aux", "occ"), P("aux", "occ"), P())
    out_specs = P("aux", "occ", None)
    return jax.shard_map(shards, mesh=mesh, in_specs=in_specs, out_specs=out_specs, check_vma=False)
```

```python
import math

import jax
import jax.numpy as jnp
from jax import lax
from jax.experimental import pallas as pl
from jax.experimental.pallas import tpu as pltpu
from jax.sharding import PartitionSpec as P

MESH = pl.DeviceIdType.MESH
NX, NC, NY, NZ = 4, 2, 4, 8
NOCC = NX * NC
BLOCK = 128
SLOTS = 4
ORB = 256
AUX = 64
CHUNK = 16
SUB = CHUNK // 2
CHUNKS = BLOCK // CHUNK
FULL = CHUNKS - 1
PHASES = FULL + 2
SPLIT = FULL - 1
QD = AUX // NOCC
DEPTH = QD * ORB
START = (*range(0, BLOCK - CHUNK + 1, CHUNK), BLOCK - SUB, BLOCK)
Y_STEPS = (2, 1, 3)
Z_STEPS = (4, 3, 5, 2, 6, 1, 7)
STEPS = ((2, 0), (2, 1), (1, 0), (3, 0), (1, 1), (3, 1), (0, 1))
PARTNERS = range(len(STEPS))
MATE = len(STEPS) - 1
HALF = CHUNKS // 2


def kernel(
    three_ref, coeff_ref, mask_ref, list_ref, count_ref, order_ref, out_ref,
    tbuf, cbuf, cm, sbuf, xbuf, ssub, xsub, wbuf, wsub, rbuf, hbuf, early, early_c, early_y, early_z, late, late_c, late_y, late_z, last, last_c, last_y, last_z, split_y, split_z, b1, b2, fsend, frecv,
    tsem, fsem, csem, xss, xrs, css, crs, yss, yrs, zss, zrs, szs, szr, sys_, syr, fss, frs,
):
    occ, aux = lax.axis_index("occ"), lax.axis_index("aux")
    x, c = occ // NC, occ % NC
    y, z = aux // NZ, aux % NZ

    def occ_to(e):
        return ((x + STEPS[e][0]) % NX) * NC + (c + STEPS[e][1]) % NC

    def occ_from(e):
        return ((x + NX - STEPS[e][0]) % NX) * NC + (c + STEPS[e][1]) % NC

    def at_occ(o):
        return (aux, o)

    def at_y(i):
        return (((y + Y_STEPS[i]) % NY) * NZ + z, occ)

    def at_z(i):
        return (y * NZ + (z + Z_STEPS[i]) % NZ, occ)

    barrier = pltpu.get_barrier_semaphore()
    for e in PARTNERS:
        pl.semaphore_signal(barrier, inc=1, device_id=at_occ(occ_to(e)), device_id_type=MESH)
    for i in range(NY - 1):
        pl.semaphore_signal(barrier, inc=1, device_id=at_y(i), device_id_type=MESH)
    for i in range(NZ - 1):
        pl.semaphore_signal(barrier, inc=1, device_id=at_z(i), device_id_type=MESH)

    def rows(t):
        return pl.ds(pl.multiple_of(t * CHUNK, CHUNK), CHUNK)

    def load(t):
        return pltpu.make_async_copy(three_ref.at[:, :, rows(t), :], tbuf.at[t], tsem.at[t])

    def load_first(d):
        at = pl.ds(pl.multiple_of(d * QD, QD), QD)
        return pltpu.make_async_copy(three_ref.at[:, at, :CHUNK, :], tbuf.at[0, :, at], fsem.at[d])

    def x_ends(e, t, sender):
        if isinstance(t, int) and t >= FULL:
            return ssub.at[e, t - FULL], xsub.at[t - FULL, sender]
        return sbuf.at[e, rows(t)], xbuf.at[sender, rows(t)]

    def x_copy(e, t):
        source, target = x_ends(e, t, occ)
        return pltpu.make_async_remote_copy(
            src_ref=source, dst_ref=target,
            send_sem=xss.at[e, t], recv_sem=xrs.at[e, t],
            device_id=at_occ(occ_to(e)), device_id_type=MESH,
        )

    def x_arrival(e, t):
        source, target = x_ends(e, t, occ_from(e))
        return pltpu.make_async_remote_copy(
            src_ref=source, dst_ref=target,
            send_sem=xss.at[e, t], recv_sem=xrs.at[e, t],
            device_id=at_occ(occ_to(e)), device_id_type=MESH,
        )

    def packs(t):
        if t < HALF:
            return early.at[t], early_c.at[t], early_y.at[t], early_z.at[t]
        if t < FULL:
            return late.at[t - HALF], late_c.at[t - HALF], late_y.at[t - HALF], late_z.at[t - HALF]
        return last.at[t - FULL], last_c.at[t - FULL], last_y.at[t - FULL], last_z.at[t - FULL]

    def group_of(i):
        return (y + Y_STEPS[i]) % NY if i < NY - 1 else y

    def c_copy(t, i):
        pack, crecv, _, _ = packs(t)
        at = group_of(i)
        return pltpu.make_async_remote_copy(
            src_ref=pack.at[1 - c, at], dst_ref=crecv.at[at],
            send_sem=css.at[t, i], recv_sem=crs.at[t, i],
            device_id=at_occ(occ_to(MATE)), device_id_type=MESH,
        )

    def y_copy(t, i):
        pack, _, yrecv, _ = packs(t)
        source, target = pack.at[c, group_of(i)], yrecv.at[i]
        if t == SPLIT:
            source, target = source.at[:, :CHUNK], target.at[:, :CHUNK]
        return pltpu.make_async_remote_copy(
            src_ref=source, dst_ref=target,
            send_sem=yss.at[t, i], recv_sem=yrs.at[t, i],
            device_id=at_y(i), device_id_type=MESH,
        )

    def z_copy(t, i):
        pack, _, _, zrecv = packs(t)
        source, target = pack.at[c, y, (z + Z_STEPS[i]) % NZ], zrecv.at[i]
        if t == SPLIT:
            source, target = source.at[:CHUNK], target.at[:CHUNK]
        return pltpu.make_async_remote_copy(
            src_ref=source, dst_ref=target,
            send_sem=zss.at[t, i], recv_sem=zrs.at[t, i],
            device_id=at_z(i), device_id_type=MESH,
        )

    def split_z_copy(i):
        return pltpu.make_async_remote_copy(
            src_ref=packs(SPLIT)[0].at[c, :, (z + Z_STEPS[i]) % NZ, CHUNK:], dst_ref=split_z.at[i],
            send_sem=szs.at[i], recv_sem=szr.at[i],
            device_id=at_z(i), device_id_type=MESH,
        )

    def split_y_copy(i):
        return pltpu.make_async_remote_copy(
            src_ref=packs(SPLIT)[0].at[c, group_of(i), z, CHUNK:], dst_ref=split_y.at[i],
            send_sem=sys_.at[i], recv_sem=syr.at[i],
            device_id=at_y(i), device_id_type=MESH,
        )

    def loop(n, body):
        def step(i, carry):
            body(i)
            return carry

        lax.fori_loop(0, n, step, 0)

    coeff_copy = pltpu.make_async_copy(coeff_ref, cbuf, csem)
    coeff_copy.start()
    for e in PARTNERS:
        load_first(occ_to(e)).start()
    load_first(occ).start()

    group = lax.broadcasted_iota(jnp.int32, (1, ORB), 1) // (ORB // NOCC)
    coeff_copy.wait()
    for s in range(SLOTS):
        n = list_ref[0, s]
        live = (s < count_ref[0, 0]).astype(jnp.int32)
        column = jnp.zeros((1, ORB), jnp.int32)
        for o in range(NOCC):
            column = jnp.where(group == o, mask_ref[n, o] * mask_ref[occ, o] * live, column)
        cm[pl.ds(s * BLOCK, BLOCK), :] = (cbuf[n].astype(jnp.float32) * column.astype(jnp.float32)).astype(jnp.bfloat16)

    def half_rows(t, dest):
        first = pl.multiple_of(dest * QD, QD)
        left = jnp.concatenate(
            [tbuf[t, s, pl.ds(first, QD)].reshape(QD * CHUNK, BLOCK) for s in range(SLOTS)], axis=1
        )
        return jnp.dot(left, cm[...], preferred_element_type=jnp.float32)

    def half(t, dest, target):
        value = half_rows(t, dest).astype(jnp.bfloat16)
        for q in range(QD):
            target[rows(t), pl.ds(q * ORB, ORB)] = value[q * CHUNK : (q + 1) * CHUNK]

    def half_last(dest, targets):
        value = half_rows(FULL, dest).reshape(QD, 2, SUB, ORB)
        for s, target in enumerate(targets):
            for q in range(QD // 2):
                pair = jnp.concatenate([value[q, s], value[q + QD // 2, s]], axis=0)
                target[:, q * ORB : (q + 1) * ORB] = pair.astype(jnp.bfloat16)

    def send(e, t):
        half(t, occ_to(e), sbuf.at[e])
        x_copy(e, t).start()

    for e in PARTNERS:
        load_first(occ_to(e)).wait()
        half(0, occ_to(e), sbuf.at[e])
        if e == 3:
            lax.fori_loop(1, CHUNKS, lambda t, v: (load(t).start(), v)[1], 0)
            pl.semaphore_wait(barrier, len(STEPS) + NY - 1 + NZ - 1)
            for i in range(e):
                x_copy(i, 0).start()
        if e >= 3:
            x_copy(e, 0).start()
    load_first(occ).wait()
    half(0, occ, xbuf.at[occ])

    def produce(t, carry):
        load(t).wait()
        for e in PARTNERS:
            send(e, t)
        half(t, occ, xbuf.at[occ])
        return carry

    lax.fori_loop(1, FULL, produce, 0)
    load(FULL).wait()
    for e in PARTNERS:
        half_last(occ_to(e), (ssub.at[e, 0], ssub.at[e, 1]))
        x_copy(e, FULL).start()
    for e in PARTNERS:
        x_copy(e, FULL + 1).start()
    half_last(occ, (xsub.at[0, occ], xsub.at[1, occ]))

    def pair_sums(t):
        for e in PARTNERS:
            x_arrival(e, t).wait_recv()
        height = START[t + 1] - START[t]
        if t < FULL:
            left = xbuf[:, t * CHUNK : (t + 1) * CHUNK, :].reshape(BLOCK, DEPTH)
            for i in range(QD):
                wbuf[t // 2, i * ORB : (i + 1) * ORB, t % 2 * BLOCK : (t % 2 + 1) * BLOCK] = left[:, i * ORB : (i + 1) * ORB].T
            for u in range(t // 2 + 1):
                value = jnp.dot(left, wbuf[u], preferred_element_type=jnp.float32)
                rbuf[2 * u] = value[:, :BLOCK].reshape(NOCC, CHUNK, BLOCK)
                rbuf[2 * u + 1] = value[:, BLOCK:].reshape(NOCC, CHUNK, BLOCK)
        else:
            left = xsub[t - FULL].reshape(BLOCK, DEPTH // 2)
            for i in range(QD // 2):
                wsub[t - FULL, i * ORB : (i + 1) * ORB, :] = left[:, i * ORB : (i + 1) * ORB].T

            def halves(value):
                value = value.reshape(NOCC, 2, SUB, value.shape[1])
                return value[:, 0], value[:, 1]

            for u in range(CHUNKS // 2):
                wide = slice(0, 2 * BLOCK if 2 * u + 1 < FULL else BLOCK)
                low = jnp.dot(left, wbuf[u, : DEPTH // 2, wide], preferred_element_type=jnp.float32)
                high = jnp.dot(left, wbuf[u, DEPTH // 2 :, wide], preferred_element_type=jnp.float32)
                value = halves(low)[0] + halves(high)[1]
                rbuf[2 * u, :, :SUB] = value[:, :, :BLOCK]
                if 2 * u + 1 < FULL:
                    rbuf[2 * u + 1, :, :SUB] = value[:, :, BLOCK:]
            low, high = halves(jnp.dot(left, wsub[0], preferred_element_type=jnp.float32))
            value = low + pltpu.roll(high, BLOCK - SUB, 2)
            if t > FULL:
                low, high = halves(jnp.dot(left, wsub[1], preferred_element_type=jnp.float32))
                lane = lax.broadcasted_iota(jnp.int32, (NOCC, SUB, BLOCK), 2)
                value = jnp.where(lane % CHUNK < SUB, value, pltpu.roll(low, SUB, 2) + high)
            rbuf[FULL, :, :SUB] = value

        if 2 <= t < PHASES - 1:
            after_y(t - 2)

        segment = lax.broadcasted_iota(jnp.int32, (height, BLOCK), 1) // CHUNK

        for d in (1, 2, 4):
            low = segment & d == 0
            for m in range(NOCC):
                for i in range(CHUNKS):
                    if i & d == 0:
                        one, two = rbuf[i, m, :height], rbuf[i + d, m, :height]
                        first = jnp.where(low, one, pltpu.roll(two, d * CHUNK, 1))
                        second = jnp.where(low, pltpu.roll(one, BLOCK - d * CHUNK, 1), two)
                        if d < 4:
                            rbuf[i, m, :height], rbuf[i + d, m, :height] = first, second
                        else:
                            hbuf[m, i, :height], hbuf[m, i + d, :height] = first, second

        pack = packs(t)[0]
        for i in range(NY):
            group = group_of(i)
            for k in range(NC * NZ):
                at, parity = k // NC, k % NC
                o = order_ref[NC * NZ * group + k]
                m, n = o >> 3, o & 7
                if t < HALF:
                    turned = pltpu.roll(hbuf[n, m], BLOCK // 2, 1)
                    pack[parity, group, at] = jnp.where(segment < HALF, hbuf[m, n], turned)
                else:
                    pack[parity, group, at, :height] = hbuf[m, n, :height]
                    pack[parity, group, at, height:] = hbuf[n, m, :height]
            c_copy(t, i).start()

    def after_core(t):
        pack, crecv, _, _ = packs(t)
        for i in range(NY):
            at = group_of(i)
            c_copy(t, i).wait_recv()
            pack[c, at] = pack[c, at] + crecv[at]
            if i < NY - 1:
                y_copy(t, i).start()
        if t == SPLIT:
            for i in range(NZ - 1):
                split_z_copy(i).start()

    def after_y(t):
        pack, _, yrecv, _ = packs(t)
        height = CHUNK if t == SPLIT else pack.shape[-2]
        for i in range(NY - 1):
            y_copy(t, i).wait_recv()
        total = pack[c, y, :, :height]
        for i in range(NY - 1):
            total = total + yrecv[i, :, :height]
        pack[c, y, :, :height] = total
        for i in range(NZ - 1):
            z_copy(t, i).start()

    def after_split_z():
        pack = packs(SPLIT)[0]
        for i in range(NZ - 1):
            split_z_copy(i).wait_recv()
        total = pack[c, :, z, CHUNK:]
        for i in range(NZ - 1):
            total = total + split_z[i]
        pack[c, :, z, CHUNK:] = total
        for i in range(NY - 1):
            split_y_copy(i).start()

    def after_split_y():
        for i in range(NY - 1):
            split_y_copy(i).wait_recv()
        total = packs(SPLIT)[0][c, y, z, CHUNK:]
        for i in range(NY - 1):
            total = total + split_y[i]
        b2[START[SPLIT] : START[SPLIT + 1], :] = total

    def after_z(t):
        pack, _, _, zrecv = packs(t)
        rows_in = CHUNK if t == SPLIT else pack.shape[-2]
        for i in range(NZ - 1):
            z_copy(t, i).wait_recv()
        total = pack[c, y, z, :rows_in]
        for i in range(NZ - 1):
            total = total + zrecv[i, :rows_in]
        height = START[t + 1] - START[t]
        b1[START[t] : START[t + 1], :] = total[:height]
        if t != SPLIT:
            b2[START[t] : START[t + 1], :] = pltpu.roll(total, BLOCK // 2, 1) if t < HALF else total[height:]

    def sent(t):
        for e in PARTNERS:
            x_copy(e, t).wait_send()
        for i in range(NY):
            c_copy(t, i).wait_send()
        for i in range(NY - 1):
            y_copy(t, i).wait_send()
        for i in range(NZ - 1):
            z_copy(t, i).wait_send()
        if t == SPLIT:
            for i in range(NZ - 1):
                split_z_copy(i).wait_send()
            for i in range(NY - 1):
                split_y_copy(i).wait_send()

    for t in range(PHASES):
        pair_sums(t)
        if 3 <= t < PHASES - 1:
            after_z(t - 3)
        after_core(t)
        if 3 <= t < PHASES - 1:
            sent(t - 3)
    after_y(PHASES - 3)
    after_z(PHASES - 4)
    after_y(PHASES - 2)
    sent(PHASES - 4)
    after_y(PHASES - 1)
    after_split_z()
    after_z(PHASES - 3)
    after_z(PHASES - 2)
    after_split_y()
    sent(PHASES - 3)
    sent(PHASES - 2)
    after_z(PHASES - 1)

    p = lax.broadcasted_iota(jnp.int32, (BLOCK, BLOCK), 0)
    q = lax.broadcasted_iota(jnp.int32, (BLOCK, BLOCK), 1)
    own_end = jnp.where(p < START[FULL], (p // CHUNK + 1) * CHUNK, (p // SUB + 1) * SUB)
    whole = jnp.where(q < own_end, b1[...], b2[...].T)
    fsend[...] = whole.reshape(NOCC, CHUNK, BLOCK)

    def f_copy(e):
        return pltpu.make_async_remote_copy(
            src_ref=fsend.at[occ_to(e)], dst_ref=frecv.at[occ],
            send_sem=fss.at[e], recv_sem=frs.at[e],
            device_id=at_occ(occ_to(e)), device_id_type=MESH,
        )

    for e in PARTNERS:
        f_copy(e).start()
    frecv[occ] = fsend[occ]

    sent(PHASES - 1)
    for e in PARTNERS:
        f_copy(e).wait()
    scale = 1.0 / math.sqrt(AUX * NY * NZ * ORB)
    for parity in range(NC):
        total = frecv[parity]
        for i in range(1, NX):
            total = total + frecv[NC * i + parity]
        out_ref[parity] = total * scale


def shards(three_index, occ_coeff, occ_mask, screen_list, screen_count, owner_order):
    f32, bf16, dma = jnp.float32, jnp.bfloat16, pltpu.SemaphoreType.DMA
    smem = pl.BlockSpec(memory_space=pltpu.SMEM)
    anywhere = pl.BlockSpec(memory_space=pl.ANY)
    return pl.pallas_call(
        kernel,
        out_shape=jax.ShapeDtypeStruct((NC, CHUNK, BLOCK), f32),
        in_specs=[anywhere, anywhere, smem, smem, smem, smem],
        out_specs=pl.BlockSpec(memory_space=pltpu.VMEM),
        scratch_shapes=[
            pltpu.VMEM((CHUNKS, SLOTS, AUX, CHUNK, BLOCK), bf16),
            pltpu.VMEM((NOCC, BLOCK, ORB), bf16),
            pltpu.VMEM((SLOTS * BLOCK, ORB), bf16),
            pltpu.VMEM((len(STEPS), BLOCK, DEPTH), bf16),
            pltpu.VMEM((NOCC, BLOCK, DEPTH), bf16),
            pltpu.VMEM((len(STEPS), 2, CHUNK, DEPTH // 2), bf16),
            pltpu.VMEM((2, NOCC, CHUNK, DEPTH // 2), bf16),
            pltpu.VMEM((CHUNKS // 2, DEPTH, 2 * BLOCK), bf16),
            pltpu.VMEM((2, DEPTH // 2, BLOCK), bf16),
            pltpu.VMEM((CHUNKS, NOCC, CHUNK, BLOCK), f32),
            pltpu.VMEM((NOCC, NOCC, CHUNK, BLOCK), f32),
            *(
                pltpu.VMEM((count, *lead, height, BLOCK), f32)
                for count, height in ((HALF, CHUNK), (FULL - HALF, 2 * CHUNK), (2, CHUNK))
                for lead in ((NC, NY, NZ), (NY, NZ), (NY - 1, NZ), (NZ - 1,))
            ),
            pltpu.VMEM((NY - 1, CHUNK, BLOCK), f32),
            pltpu.VMEM((NZ - 1, NY, CHUNK, BLOCK), f32),
            pltpu.VMEM((BLOCK, BLOCK), f32),
            pltpu.VMEM((BLOCK, BLOCK), f32),
            pltpu.VMEM((NOCC, CHUNK, BLOCK), f32),
            pltpu.VMEM((NOCC, CHUNK, BLOCK), f32),
            dma((CHUNKS,)),
            dma((NOCC,)),
            dma,
            dma((len(STEPS), PHASES)),
            dma((len(STEPS), PHASES)),
            dma((PHASES, NY)),
            dma((PHASES, NY)),
            dma((PHASES, NY - 1)),
            dma((PHASES, NY - 1)),
            dma((PHASES, NZ - 1)),
            dma((PHASES, NZ - 1)),
            dma((NZ - 1,)),
            dma((NZ - 1,)),
            dma((NY - 1,)),
            dma((NY - 1,)),
            dma((len(STEPS),)),
            dma((len(STEPS),)),
        ],
        compiler_params=pltpu.CompilerParams(
            collective_id=0, has_side_effects=True, vmem_limit_bytes=56 * 1024 * 1024
        ),
        name="exchange",
    )(three_index, occ_coeff.reshape(NOCC, BLOCK, ORB), occ_mask, screen_list, screen_count, owner_order)


def solution(mesh):
    in_specs = (P("occ", "aux", None, None), P(), P(), P("aux", "occ"), P("aux", "occ"), P())
    out_specs = P("aux", "occ", None)
    return jax.shard_map(shards, mesh=mesh, in_specs=in_specs, out_specs=out_specs, check_vma=False)
```

```python
import math

import jax
import jax.numpy as jnp
from jax import lax
from jax.experimental import pallas as pl
from jax.experimental.pallas import tpu as pltpu
from jax.sharding import PartitionSpec as P

MESH = pl.DeviceIdType.MESH
NX, NC, NY, NZ = 4, 2, 4, 8
NOCC = NX * NC
BLOCK = 128
SLOTS = 4
ORB = 256
AUX = 64
CHUNK = 16
SUB = CHUNK // 2
CHUNKS = BLOCK // CHUNK
FULL = CHUNKS - 1
PHASES = FULL + 2
SPLIT = FULL - 1
QD = AUX // NOCC
DEPTH = QD * ORB
START = (*range(0, BLOCK - CHUNK + 1, CHUNK), BLOCK - SUB, BLOCK)
Y_STEPS = (2, 1, 3)
Z_STEPS = (4, 3, 5, 2, 6, 1, 7)
STEPS = ((2, 0), (2, 1), (1, 0), (3, 0), (1, 1), (3, 1), (0, 1))
PARTNERS = range(len(STEPS))
MATE = len(STEPS) - 1
HALF = CHUNKS // 2


def kernel(
    three_ref, coeff_ref, mask_ref, list_ref, count_ref, order_ref, frecv,
    tbuf, cbuf, cm, sbuf, xbuf, ssub, xsub, wbuf, wsub, rbuf, hbuf, early, early_c, early_y, early_z, late, late_c, late_y, late_z, last, last_c, last_y, last_z, split_y, split_z, b1, b2, fsend,
    tsem, fsem, csem, xss, xrs, css, crs, yss, yrs, zss, zrs, szs, szr, sys_, syr, fss, frs,
):
    occ, aux = lax.axis_index("occ"), lax.axis_index("aux")
    x, c = occ // NC, occ % NC
    y, z = aux // NZ, aux % NZ

    def occ_to(e):
        return ((x + STEPS[e][0]) % NX) * NC + (c + STEPS[e][1]) % NC

    def occ_from(e):
        return ((x + NX - STEPS[e][0]) % NX) * NC + (c + STEPS[e][1]) % NC

    def at_occ(o):
        return (aux, o)

    def at_y(i):
        return (((y + Y_STEPS[i]) % NY) * NZ + z, occ)

    def at_z(i):
        return (y * NZ + (z + Z_STEPS[i]) % NZ, occ)

    barrier = pltpu.get_barrier_semaphore()
    for e in PARTNERS:
        pl.semaphore_signal(barrier, inc=1, device_id=at_occ(occ_to(e)), device_id_type=MESH)
    for i in range(NY - 1):
        pl.semaphore_signal(barrier, inc=1, device_id=at_y(i), device_id_type=MESH)
    for i in range(NZ - 1):
        pl.semaphore_signal(barrier, inc=1, device_id=at_z(i), device_id_type=MESH)

    def rows(t):
        return pl.ds(pl.multiple_of(t * CHUNK, CHUNK), CHUNK)

    def load(t):
        return pltpu.make_async_copy(three_ref.at[:, :, rows(t), :], tbuf.at[t], tsem.at[t])

    def load_first(d):
        at = pl.ds(pl.multiple_of(d * QD, QD), QD)
        return pltpu.make_async_copy(three_ref.at[:, at, :CHUNK, :], tbuf.at[0, :, at], fsem.at[d])

    def x_ends(e, t, sender):
        if isinstance(t, int) and t >= FULL:
            return ssub.at[e, t - FULL], xsub.at[t - FULL, sender]
        return sbuf.at[e, rows(t)], xbuf.at[sender, rows(t)]

    def x_copy(e, t):
        source, target = x_ends(e, t, occ)
        return pltpu.make_async_remote_copy(
            src_ref=source, dst_ref=target,
            send_sem=xss.at[e, t], recv_sem=xrs.at[e, t],
            device_id=at_occ(occ_to(e)), device_id_type=MESH,
        )

    def x_arrival(e, t):
        source, target = x_ends(e, t, occ_from(e))
        return pltpu.make_async_remote_copy(
            src_ref=source, dst_ref=target,
            send_sem=xss.at[e, t], recv_sem=xrs.at[e, t],
            device_id=at_occ(occ_to(e)), device_id_type=MESH,
        )

    def packs(t):
        if t < HALF:
            return early.at[t], early_c.at[t], early_y.at[t], early_z.at[t]
        if t < FULL:
            return late.at[t - HALF], late_c.at[t - HALF], late_y.at[t - HALF], late_z.at[t - HALF]
        return last.at[t - FULL], last_c.at[t - FULL], last_y.at[t - FULL], last_z.at[t - FULL]

    def group_of(i):
        return (y + Y_STEPS[i]) % NY if i < NY - 1 else y

    def c_copy(t, i):
        pack, crecv, _, _ = packs(t)
        at = group_of(i)
        return pltpu.make_async_remote_copy(
            src_ref=pack.at[1 - c, at], dst_ref=crecv.at[at],
            send_sem=css.at[t, i], recv_sem=crs.at[t, i],
            device_id=at_occ(occ_to(MATE)), device_id_type=MESH,
        )

    def y_copy(t, i):
        pack, _, yrecv, _ = packs(t)
        source, target = pack.at[c, group_of(i)], yrecv.at[i]
        if t == SPLIT:
            source, target = source.at[:, :CHUNK], target.at[:, :CHUNK]
        return pltpu.make_async_remote_copy(
            src_ref=source, dst_ref=target,
            send_sem=yss.at[t, i], recv_sem=yrs.at[t, i],
            device_id=at_y(i), device_id_type=MESH,
        )

    def z_copy(t, i):
        pack, _, _, zrecv = packs(t)
        source, target = pack.at[c, y, (z + Z_STEPS[i]) % NZ], zrecv.at[i]
        if t == SPLIT:
            source, target = source.at[:CHUNK], target.at[:CHUNK]
        return pltpu.make_async_remote_copy(
            src_ref=source, dst_ref=target,
            send_sem=zss.at[t, i], recv_sem=zrs.at[t, i],
            device_id=at_z(i), device_id_type=MESH,
        )

    def split_z_copy(i):
        return pltpu.make_async_remote_copy(
            src_ref=packs(SPLIT)[0].at[c, :, (z + Z_STEPS[i]) % NZ, CHUNK:], dst_ref=split_z.at[i],
            send_sem=szs.at[i], recv_sem=szr.at[i],
            device_id=at_z(i), device_id_type=MESH,
        )

    def split_y_copy(i):
        return pltpu.make_async_remote_copy(
            src_ref=packs(SPLIT)[0].at[c, group_of(i), z, CHUNK:], dst_ref=split_y.at[i],
            send_sem=sys_.at[i], recv_sem=syr.at[i],
            device_id=at_y(i), device_id_type=MESH,
        )

    def loop(n, body):
        def step(i, carry):
            body(i)
            return carry

        lax.fori_loop(0, n, step, 0)

    coeff_copy = pltpu.make_async_copy(coeff_ref, cbuf, csem)
    coeff_copy.start()
    for e in PARTNERS:
        load_first(occ_to(e)).start()
    load_first(occ).start()

    group = lax.broadcasted_iota(jnp.int32, (1, ORB), 1) // (ORB // NOCC)
    coeff_copy.wait()
    for s in range(SLOTS):
        n = list_ref[0, s]
        live = (s < count_ref[0, 0]).astype(jnp.int32)
        column = jnp.zeros((1, ORB), jnp.int32)
        for o in range(NOCC):
            column = jnp.where(group == o, mask_ref[n, o] * mask_ref[occ, o] * live, column)
        cm[pl.ds(s * BLOCK, BLOCK), :] = (cbuf[n].astype(jnp.float32) * column.astype(jnp.float32)).astype(jnp.bfloat16)

    def half_rows(t, dest):
        first = pl.multiple_of(dest * QD, QD)
        left = jnp.concatenate(
            [tbuf[t, s, pl.ds(first, QD)].reshape(QD * CHUNK, BLOCK) for s in range(SLOTS)], axis=1
        )
        return jnp.dot(left, cm[...], preferred_element_type=jnp.float32)

    def half(t, dest, target):
        value = half_rows(t, dest).astype(jnp.bfloat16)
        for q in range(QD):
            target[rows(t), pl.ds(q * ORB, ORB)] = value[q * CHUNK : (q + 1) * CHUNK]

    def half_last(dest, targets):
        value = half_rows(FULL, dest).reshape(QD, 2, SUB, ORB)
        for s, target in enumerate(targets):
            for q in range(QD // 2):
                pair = jnp.concatenate([value[q, s], value[q + QD // 2, s]], axis=0)
                target[:, q * ORB : (q + 1) * ORB] = pair.astype(jnp.bfloat16)

    def send(e, t):
        half(t, occ_to(e), sbuf.at[e])
        x_copy(e, t).start()

    for e in PARTNERS:
        load_first(occ_to(e)).wait()
        half(0, occ_to(e), sbuf.at[e])
        if e == 3:
            lax.fori_loop(1, CHUNKS, lambda t, v: (load(t).start(), v)[1], 0)
            pl.semaphore_wait(barrier, len(STEPS) + NY - 1 + NZ - 1)
            for i in range(e):
                x_copy(i, 0).start()
        if e >= 3:
            x_copy(e, 0).start()
    load_first(occ).wait()
    half(0, occ, xbuf.at[occ])

    def produce(t, carry):
        load(t).wait()
        for e in PARTNERS:
            send(e, t)
        half(t, occ, xbuf.at[occ])
        return carry

    lax.fori_loop(1, FULL, produce, 0)
    load(FULL).wait()
    for e in PARTNERS:
        half_last(occ_to(e), (ssub.at[e, 0], ssub.at[e, 1]))
        x_copy(e, FULL).start()
    for e in PARTNERS:
        x_copy(e, FULL + 1).start()
    half_last(occ, (xsub.at[0, occ], xsub.at[1, occ]))

    def pair_sums(t):
        for e in PARTNERS:
            x_arrival(e, t).wait_recv()
        height = START[t + 1] - START[t]
        if t < FULL:
            left = xbuf[:, t * CHUNK : (t + 1) * CHUNK, :].reshape(BLOCK, DEPTH)
            for i in range(QD):
                wbuf[t // 2, i * ORB : (i + 1) * ORB, t % 2 * BLOCK : (t % 2 + 1) * BLOCK] = left[:, i * ORB : (i + 1) * ORB].T
            for u in range(t // 2 + 1):
                value = jnp.dot(left, wbuf[u], preferred_element_type=jnp.float32)
                rbuf[2 * u] = value[:, :BLOCK].reshape(NOCC, CHUNK, BLOCK)
                rbuf[2 * u + 1] = value[:, BLOCK:].reshape(NOCC, CHUNK, BLOCK)
        else:
            left = xsub[t - FULL].reshape(BLOCK, DEPTH // 2)
            for i in range(QD // 2):
                wsub[t - FULL, i * ORB : (i + 1) * ORB, :] = left[:, i * ORB : (i + 1) * ORB].T

            def halves(value):
                value = value.reshape(NOCC, 2, SUB, value.shape[1])
                return value[:, 0], value[:, 1]

            for u in range(CHUNKS // 2):
                wide = slice(0, 2 * BLOCK if 2 * u + 1 < FULL else BLOCK)
                low = jnp.dot(left, wbuf[u, : DEPTH // 2, wide], preferred_element_type=jnp.float32)
                high = jnp.dot(left, wbuf[u, DEPTH // 2 :, wide], preferred_element_type=jnp.float32)
                value = halves(low)[0] + halves(high)[1]
                rbuf[2 * u, :, :SUB] = value[:, :, :BLOCK]
                if 2 * u + 1 < FULL:
                    rbuf[2 * u + 1, :, :SUB] = value[:, :, BLOCK:]
            low, high = halves(jnp.dot(left, wsub[0], preferred_element_type=jnp.float32))
            value = low + pltpu.roll(high, BLOCK - SUB, 2)
            if t > FULL:
                low, high = halves(jnp.dot(left, wsub[1], preferred_element_type=jnp.float32))
                lane = lax.broadcasted_iota(jnp.int32, (NOCC, SUB, BLOCK), 2)
                value = jnp.where(lane % CHUNK < SUB, value, pltpu.roll(low, SUB, 2) + high)
            rbuf[FULL, :, :SUB] = value

        if 2 <= t < PHASES - 1:
            after_y(t - 2)

        segment = lax.broadcasted_iota(jnp.int32, (height, BLOCK), 1) // CHUNK

        for d in (1, 2, 4):
            low = segment & d == 0
            for m in range(NOCC):
                for i in range(CHUNKS):
                    if i & d == 0:
                        one, two = rbuf[i, m, :height], rbuf[i + d, m, :height]
                        first = jnp.where(low, one, pltpu.roll(two, d * CHUNK, 1))
                        second = jnp.where(low, pltpu.roll(one, BLOCK - d * CHUNK, 1), two)
                        if d < 4:
                            rbuf[i, m, :height], rbuf[i + d, m, :height] = first, second
                        else:
                            hbuf[m, i, :height], hbuf[m, i + d, :height] = first, second

        pack = packs(t)[0]
        for i in range(NY):
            group = group_of(i)
            for k in range(NC * NZ):
                at, parity = k // NC, k % NC
                o = order_ref[NC * NZ * group + k]
                m, n = o >> 3, o & 7
                if t < HALF:
                    turned = pltpu.roll(hbuf[n, m], BLOCK // 2, 1)
                    pack[parity, group, at] = jnp.where(segment < HALF, hbuf[m, n], turned)
                else:
                    pack[parity, group, at, :height] = hbuf[m, n, :height]
                    pack[parity, group, at, height:] = hbuf[n, m, :height]
            c_copy(t, i).start()

    def after_core(t):
        pack, crecv, _, _ = packs(t)
        for i in range(NY):
            at = group_of(i)
            c_copy(t, i).wait_recv()
            pack[c, at] = pack[c, at] + crecv[at]
            if i < NY - 1:
                y_copy(t, i).start()
        if t == SPLIT:
            for i in range(NZ - 1):
                split_z_copy(i).start()

    def after_y(t):
        pack, _, yrecv, _ = packs(t)
        height = CHUNK if t == SPLIT else pack.shape[-2]
        for i in range(NY - 1):
            y_copy(t, i).wait_recv()
        total = pack[c, y, :, :height]
        for i in range(NY - 1):
            total = total + yrecv[i, :, :height]
        pack[c, y, :, :height] = total
        for i in range(NZ - 1):
            z_copy(t, i).start()

    def after_split_z():
        pack = packs(SPLIT)[0]
        for i in range(NZ - 1):
            split_z_copy(i).wait_recv()
        total = pack[c, :, z, CHUNK:]
        for i in range(NZ - 1):
            total = total + split_z[i]
        pack[c, :, z, CHUNK:] = total
        for i in range(NY - 1):
            split_y_copy(i).start()

    def after_split_y():
        for i in range(NY - 1):
            split_y_copy(i).wait_recv()
        total = packs(SPLIT)[0][c, y, z, CHUNK:]
        for i in range(NY - 1):
            total = total + split_y[i]
        b2[START[SPLIT] : START[SPLIT + 1], :] = total

    def after_z(t):
        pack, _, _, zrecv = packs(t)
        rows_in = CHUNK if t == SPLIT else pack.shape[-2]
        for i in range(NZ - 1):
            z_copy(t, i).wait_recv()
        total = pack[c, y, z, :rows_in]
        for i in range(NZ - 1):
            total = total + zrecv[i, :rows_in]
        height = START[t + 1] - START[t]
        b1[START[t] : START[t + 1], :] = total[:height]
        if t != SPLIT:
            b2[START[t] : START[t + 1], :] = pltpu.roll(total, BLOCK // 2, 1) if t < HALF else total[height:]

    def sent(t):
        for e in PARTNERS:
            x_copy(e, t).wait_send()
        for i in range(NY):
            c_copy(t, i).wait_send()
        for i in range(NY - 1):
            y_copy(t, i).wait_send()
        for i in range(NZ - 1):
            z_copy(t, i).wait_send()
        if t == SPLIT:
            for i in range(NZ - 1):
                split_z_copy(i).wait_send()
            for i in range(NY - 1):
                split_y_copy(i).wait_send()

    for t in range(PHASES):
        pair_sums(t)
        if 3 <= t < PHASES - 1:
            after_z(t - 3)
        after_core(t)
        if 3 <= t < PHASES - 1:
            sent(t - 3)
    after_y(PHASES - 3)
    after_z(PHASES - 4)
    after_y(PHASES - 2)
    sent(PHASES - 4)
    after_y(PHASES - 1)
    after_split_z()
    after_z(PHASES - 3)
    after_z(PHASES - 2)
    after_split_y()
    sent(PHASES - 3)
    sent(PHASES - 2)
    after_z(PHASES - 1)

    p = lax.broadcasted_iota(jnp.int32, (BLOCK, BLOCK), 0)
    q = lax.broadcasted_iota(jnp.int32, (BLOCK, BLOCK), 1)
    own_end = jnp.where(p < START[FULL], (p // CHUNK + 1) * CHUNK, (p // SUB + 1) * SUB)
    whole = jnp.where(q < own_end, b1[...], b2[...].T)
    fsend[...] = whole.reshape(NOCC, CHUNK, BLOCK)

    def f_copy(e):
        return pltpu.make_async_remote_copy(
            src_ref=fsend.at[occ_to(e)], dst_ref=frecv.at[occ],
            send_sem=fss.at[e], recv_sem=frs.at[e],
            device_id=at_occ(occ_to(e)), device_id_type=MESH,
        )

    for e in PARTNERS:
        f_copy(e).start()
    frecv[occ] = fsend[occ]

    sent(PHASES - 1)
    for e in PARTNERS:
        f_copy(e).wait()


def add_up(parts_ref, out_ref):
    scale = 1.0 / math.sqrt(AUX * NY * NZ * ORB)
    for parity in range(NC):
        total = parts_ref[parity]
        for i in range(1, NX):
            total = total + parts_ref[NC * i + parity]
        out_ref[parity] = total * scale


def shards(three_index, occ_coeff, occ_mask, screen_list, screen_count, owner_order):
    f32, bf16, dma = jnp.float32, jnp.bfloat16, pltpu.SemaphoreType.DMA
    smem = pl.BlockSpec(memory_space=pltpu.SMEM)
    anywhere = pl.BlockSpec(memory_space=pl.ANY)
    parts = pl.pallas_call(
        kernel,
        out_shape=jax.ShapeDtypeStruct((NOCC, CHUNK, BLOCK), f32),
        in_specs=[anywhere, anywhere, smem, smem, smem, smem],
        out_specs=pl.BlockSpec(memory_space=pltpu.VMEM),
        scratch_shapes=[
            pltpu.VMEM((CHUNKS, SLOTS, AUX, CHUNK, BLOCK), bf16),
            pltpu.VMEM((NOCC, BLOCK, ORB), bf16),
            pltpu.VMEM((SLOTS * BLOCK, ORB), bf16),
            pltpu.VMEM((len(STEPS), BLOCK, DEPTH), bf16),
            pltpu.VMEM((NOCC, BLOCK, DEPTH), bf16),
            pltpu.VMEM((len(STEPS), 2, CHUNK, DEPTH // 2), bf16),
            pltpu.VMEM((2, NOCC, CHUNK, DEPTH // 2), bf16),
            pltpu.VMEM((CHUNKS // 2, DEPTH, 2 * BLOCK), bf16),
            pltpu.VMEM((2, DEPTH // 2, BLOCK), bf16),
            pltpu.VMEM((CHUNKS, NOCC, CHUNK, BLOCK), f32),
            pltpu.VMEM((NOCC, NOCC, CHUNK, BLOCK), f32),
            *(
                pltpu.VMEM((count, *lead, height, BLOCK), f32)
                for count, height in ((HALF, CHUNK), (FULL - HALF, 2 * CHUNK), (2, CHUNK))
                for lead in ((NC, NY, NZ), (NY, NZ), (NY - 1, NZ), (NZ - 1,))
            ),
            pltpu.VMEM((NY - 1, CHUNK, BLOCK), f32),
            pltpu.VMEM((NZ - 1, NY, CHUNK, BLOCK), f32),
            pltpu.VMEM((BLOCK, BLOCK), f32),
            pltpu.VMEM((BLOCK, BLOCK), f32),
            pltpu.VMEM((NOCC, CHUNK, BLOCK), f32),
            dma((CHUNKS,)),
            dma((NOCC,)),
            dma,
            dma((len(STEPS), PHASES)),
            dma((len(STEPS), PHASES)),
            dma((PHASES, NY)),
            dma((PHASES, NY)),
            dma((PHASES, NY - 1)),
            dma((PHASES, NY - 1)),
            dma((PHASES, NZ - 1)),
            dma((PHASES, NZ - 1)),
            dma((NZ - 1,)),
            dma((NZ - 1,)),
            dma((NY - 1,)),
            dma((NY - 1,)),
            dma((len(STEPS),)),
            dma((len(STEPS),)),
        ],
        compiler_params=pltpu.CompilerParams(
            collective_id=0, has_side_effects=True, vmem_limit_bytes=56 * 1024 * 1024
        ),
        name="exchange",
    )(three_index, occ_coeff.reshape(NOCC, BLOCK, ORB), occ_mask, screen_list, screen_count, owner_order)
    return pl.pallas_call(
        add_up,
        out_shape=jax.ShapeDtypeStruct((NC, CHUNK, BLOCK), f32),
        in_specs=[pl.BlockSpec(memory_space=pltpu.VMEM)],
        out_specs=pl.BlockSpec(memory_space=pltpu.VMEM),
        name="add_up",
    )(parts)


def solution(mesh):
    in_specs = (P("occ", "aux", None, None), P(), P(), P("aux", "occ"), P("aux", "occ"), P())
    out_specs = P("aux", "occ", None)
    return jax.shard_map(shards, mesh=mesh, in_specs=in_specs, out_specs=out_specs, check_vma=False)
```
